512 devices in a mesh: layer: 2 (over core), row: 16 (over y, x_lo), col: 16 (over x_hi, z).
Axes of the slice: x: 4 (x_hi: 2, x_lo: 2; x = x_hi * 2 + x_lo), y: 8, z: 8, core: 2. Of those that a mesh axis runs over, the one named last changes fastest.
Arguments:
- amplitudes: bfloat16 [896, 73728], P('row', ('layer', 'col')), may hold values from -6 to 6
- integrals: bfloat16 [73728, 2048], P(('layer', 'row'), 'col'), may hold values from -0.0234375 to 0.0234375
- other_terms: float32 [896, 2048], P('row', 'col'), may hold values from -6 to 6
- occ_energy: float32 [896], P('row'), may hold values from -4 to -1
- virt_energy: float32 [2048], P('col'), may hold values from 0.5 to 6
Outputs:
- new_amplitudes: float32 [896, 2048], P('row', 'col')
The draws below stay inside these ranges and needn't reach their ends.
All inputs are finite; a program needn't handle non-finite values.
Results may differ from the reference program's by a relative error of at most 0.0003.
Values may be sent and summed in bfloat16 or wider, within the bound.
No kernel may reach another device: no remote copies, remote signals or barrier semaphores. Data moves between devices by JAX's collectives and lax.ppermute only.
A program may use at most 64 MiB of HBM per device.

```python
import jax
import jax.numpy as jnp

VPAIRS = 73728
PAIRS = 896
PANEL = 2048


def block_scale(stream_key, dims, shards, smallest, largest):
    loudness, own = 1.0, jax.random.fold_in(stream_key, 6)
    for position, parts in shards:
        steps = jnp.exp(jax.random.uniform(jax.random.fold_in(own, position), (parts,), jnp.float32, smallest / len(shards), largest / len(shards)))
        loudness = loudness * jnp.repeat(steps, dims[position] // parts).reshape([-1 if axis == position else 1 for axis in range(len(dims))])
    return loudness


def normal_values(key, extent, width, reach, cuts=(), kind=jnp.bfloat16):
    array = width * jax.random.normal(key, extent, jnp.float32)
    if cuts:
        array = array * block_scale(key, extent, cuts, -0.22, 0.18)
    return jnp.clip(array, -reach, reach).astype(kind)


def setup_inputs(seed: int = 0) -> dict:
    splits = jax.random.split(jax.random.key(seed), 6)
    amplitudes = normal_values(splits[0], (PAIRS, VPAIRS), 1.0, 6.0, ((0, 16), (1, 32)))
    integrals = normal_values(splits[1], (VPAIRS, PANEL), VPAIRS ** -0.5, 0.0234375, ((0, 32), (1, 16)))
    other_terms = normal_values(splits[2], (PAIRS, PANEL), 1.0, 6.0, ((0, 16), (1, 16)), jnp.float32)
    occ_energy = jnp.clip(-4.0 + 3.0 * jax.random.uniform(splits[3], (PAIRS,), jnp.float32) ** block_scale(splits[3], (PAIRS,), ((0, 16),), -0.2, 0.2), -4.0, -1.0)
    virt_energy = jnp.clip(0.5 + 5.5 * jax.random.uniform(splits[4], (PANEL,), jnp.float32) ** block_scale(splits[4], (PANEL,), ((0, 16),), -0.2, 0.2), 0.5, 6.0)
    return {"amplitudes": amplitudes, "integrals": integrals, "other_terms": other_terms, "occ_energy": occ_energy, "virt_energy": virt_energy}


def reference(amplitudes, integrals, other_terms, occ_energy, virt_energy):
    ladder = jnp.dot(amplitudes, integrals, preferred_element_type=jnp.float32)
    denominator = occ_energy[:, None] - virt_energy[None, :]
    return (ladder + other_terms) / denominator
```

```python
import jax
import jax.numpy as jnp
from jax import lax
from jax.experimental import pallas as pl
from jax.experimental.pallas import tpu as pltpu
from jax.sharding import Mesh
from jax.sharding import PartitionSpec as P

PARTS = {"l": 2, "yh": 4, "yl": 2, "xl": 2, "xh": 2, "zh": 4, "zl": 2}
FAR = ("yh", "zh")
PIECES = 16
ROWS = 56
LANES = 128
MAIN = PIECES * LANES
REST = 16
A_ROWS = 64
B_ROWS = LANES + REST
VMEM = 40 * 1024 * 1024


def pack_kernel(a_ref, b_ref, out_ref):
    lane_group = lax.broadcasted_iota(jnp.int32, (8, LANES), 1) // REST
    tail = a_ref[:, MAIN:].astype(jnp.float32)
    for s in range(PIECES):
        main = a_ref[:, s * LANES : (s + 1) * LANES].astype(jnp.float32)
        half, place = divmod(s, 8)
        rest = jnp.zeros((8, LANES), jnp.float32)
        for g in range(ROWS // 8):
            tile = tail[8 * g : 8 * g + 8, half * LANES : (half + 1) * LANES]
            shift = REST * (g - place) % LANES
            moved = pltpu.roll(tile, shift, 1) if shift else tile
            rest = jnp.where(lane_group == g, moved, rest)
        out_ref[s, 0:A_ROWS, :] = jnp.concatenate([main, rest], axis=0).astype(jnp.bfloat16)
        out_ref[s, A_ROWS : A_ROWS + LANES, :] = b_ref[s * LANES : (s + 1) * LANES, :]
        out_ref[s, A_ROWS + LANES :, :] = b_ref[MAIN + s * REST : MAIN + (s + 1) * REST, :]


def pack(a, b):
    return pl.pallas_call(
        pack_kernel,
        out_shape=jax.ShapeDtypeStruct((PIECES, A_ROWS + B_ROWS, LANES), jnp.bfloat16),
        in_specs=[pl.BlockSpec(memory_space=pltpu.VMEM)] * 2,
        out_specs=pl.BlockSpec(memory_space=pltpu.VMEM),
        compiler_params=pltpu.CompilerParams(vmem_limit_bytes=VMEM),
    )(a, b)


def multiply_kernel(place_ref, *refs):
    a_refs, b_refs, (out_ref, left, right, spread) = refs[:4], refs[4:8], refs[8:]
    my_yl, my_xl, my_xh, my_zl = (place_ref[i] for i in range(4))
    lane_group = lax.broadcasted_iota(jnp.int32, (4 * 8, LANES), 1) // REST
    tails = []
    for t in range(PIECES):
        dxh, dzl, b2, dyl = t >> 3, (t >> 2) & 1, (t >> 1) & 1, t & 1
        a_ref = a_refs[2 * dxh + dzl]
        zh = 2 * b2 + (my_yl ^ dyl)
        tail = []
        for yh in range(4):
            left[A_ROWS * yh : A_ROWS * (yh + 1), t * LANES : (t + 1) * LANES] = a_ref[4 * yh + zh]
            tail.append(a_ref[4 * yh + zh, A_ROWS - 16 :, :].astype(jnp.float32)[8:])
        tails.append(jnp.concatenate(tail, axis=0))
    spread[...] = jnp.zeros_like(spread)
    for half in range(2):
        for g in range(ROWS // 8):
            rest = jnp.zeros((4 * 8, LANES), jnp.float32)
            for place in range(8):
                shift = REST * (place - g) % LANES
                tile = tails[8 * half + place]
                moved = pltpu.roll(tile, shift, 1) if shift else tile
                rest = jnp.where(lane_group == place, moved, rest)
            for yh in range(4):
                spread[A_ROWS * yh + 8 * g : A_ROWS * yh + 8 * g + 8, half * LANES : (half + 1) * LANES] = rest[8 * yh : 8 * yh + 8]
    left[:, MAIN:] = spread[...].astype(jnp.bfloat16)

    def lay_right(same):
        for t in range(PIECES):
            dxh, dzl, b2, dyl = t >> 3, (t >> 2) & 1, (t >> 1) & 1, t & 1
            b_ref = b_refs[2 * dyl + (dzl if same else 1 - dzl)]
            yh = 2 * (my_xh ^ dxh) + b2
            for zh in range(4):
                columns = slice(zh * LANES, (zh + 1) * LANES)
                right[t * LANES : (t + 1) * LANES, columns] = b_ref[4 * yh + zh, 0:LANES, :]
                right[MAIN + t * REST : MAIN + (t + 1) * REST, columns] = b_ref[4 * yh + zh, LANES:, :]

    pl.when(my_zl == my_xl)(lambda: lay_right(True))
    pl.when(my_zl != my_xl)(lambda: lay_right(False))
    total = jnp.dot(left[...], right[...], preferred_element_type=jnp.float32)
    for yh in range(4):
        for zh in range(4):
            out_ref[4 * yh + zh] = total[A_ROWS * yh : A_ROWS * yh + ROWS, zh * LANES : (zh + 1) * LANES]


def multiply(place, a_slots, b_slots):
    depth = PIECES * (LANES + REST)
    return pl.pallas_call(
        multiply_kernel,
        out_shape=jax.ShapeDtypeStruct((PIECES, ROWS, LANES), jnp.float32),
        in_specs=[pl.BlockSpec(memory_space=pltpu.SMEM)] + [pl.BlockSpec(memory_space=pltpu.VMEM)] * 8,
        out_specs=pl.BlockSpec(memory_space=pltpu.VMEM),
        scratch_shapes=[
            pltpu.VMEM((4 * A_ROWS, depth), jnp.bfloat16),
            pltpu.VMEM((depth, 4 * LANES), jnp.bfloat16),
            pltpu.VMEM((4 * A_ROWS, 2 * LANES), jnp.float32),
        ],
        compiler_params=pltpu.CompilerParams(vmem_limit_bytes=VMEM),
    )(place, *a_slots, *b_slots)


def neighbours(block, axes):
    return [block] + [lax.ppermute(block, axes, [(i, i ^ d) for i in range(4)]) for d in (1, 2, 3)]


def body(amplitudes, integrals, other_terms, occ_energy, virt_energy):
    pieces = lax.all_to_all(pack(amplitudes, integrals), FAR, 0, 0, tiled=True)
    b_slots = neighbours(pieces[:, A_ROWS:], ("yl", "xl"))
    a_slots = neighbours(pieces[:, :A_ROWS], ("xh", "zl"))
    place = jnp.stack([lax.axis_index(n) for n in ("yl", "xl", "xh", "zl")]).astype(jnp.int32)
    partial = multiply(place, a_slots, b_slots)
    partial = lax.all_to_all(partial, FAR, 0, 0, tiled=True)
    ladder = lax.psum(jnp.sum(partial, axis=0), "l")
    denominator = occ_energy[:, None] - virt_energy[None, :]
    return (ladder + other_terms) / denominator


def solution(mesh):
    fine = Mesh(mesh.devices.reshape(tuple(PARTS.values())), tuple(PARTS))
    row, col = ("yh", "yl", "xl"), ("xh", "zh", "zl")
    in_specs = (P(row, ("l",) + col), P(("l",) + row, col), P(row, col), P(row), P(col))
    return jax.shard_map(body, mesh=fine, in_specs=in_specs, out_specs=P(row, col), check_vma=False)
```

```python
import jax
import jax.numpy as jnp
from jax import lax
from jax.experimental import pallas as pl
from jax.experimental.pallas import tpu as pltpu
from jax.sharding import Mesh
from jax.sharding import PartitionSpec as P

PARTS = {"l": 2, "yh": 4, "yl": 2, "xl": 2, "xh": 2, "zh": 4, "zl": 2}
NEAR = ("yl", "xl", "xh", "zl")
PIECES = 16
ROWS = 56
LANES = 128
MAIN = PIECES * LANES
REST = 16
A_ROWS = 64
B_ROWS = LANES + REST
VMEM = 40 * 1024 * 1024


def pack_kernel(a_ref, b_ref, out_ref):
    lane_group = lax.broadcasted_iota(jnp.int32, (8, LANES), 1) // REST
    tail = a_ref[:, MAIN:].astype(jnp.float32)
    for s in range(PIECES):
        main = a_ref[:, s * LANES : (s + 1) * LANES].astype(jnp.float32)
        half, place = divmod(s, 8)
        rest = jnp.zeros((8, LANES), jnp.float32)
        for g in range(ROWS // 8):
            tile = tail[8 * g : 8 * g + 8, half * LANES : (half + 1) * LANES]
            shift = REST * (g - place) % LANES
            moved = pltpu.roll(tile, shift, 1) if shift else tile
            rest = jnp.where(lane_group == g, moved, rest)
        out_ref[s, 0:A_ROWS, :] = jnp.concatenate([main, rest], axis=0).astype(jnp.bfloat16)
        out_ref[s, A_ROWS : A_ROWS + LANES, :] = b_ref[s * LANES : (s + 1) * LANES, :]
        out_ref[s, A_ROWS + LANES :, :] = b_ref[MAIN + s * REST : MAIN + (s + 1) * REST, :]


def pack(a, b):
    return pl.pallas_call(
        pack_kernel,
        out_shape=jax.ShapeDtypeStruct((PIECES, A_ROWS + B_ROWS, LANES), jnp.bfloat16),
        in_specs=[pl.BlockSpec(memory_space=pltpu.VMEM)] * 2,
        out_specs=pl.BlockSpec(memory_space=pltpu.VMEM),
        compiler_params=pltpu.CompilerParams(vmem_limit_bytes=VMEM),
    )(a, b)


def multiply_kernel(my_zh_ref, *refs):
    a_refs, (b_ref, out_ref, left, right, spread) = refs[:4], refs[4:]
    my_zh = my_zh_ref[0]
    lane_group = lax.broadcasted_iota(jnp.int32, (4 * 8, LANES), 1) // REST
    tails = []
    for t in range(PIECES):
        flip, b3, b0 = t >> 2, (t >> 1) & 1, t & 1
        zh = my_zh ^ flip
        b2, b1 = zh >> 1, zh & 1
        tail = []
        for r in range(4):
            piece = 4 * r + 2 * b3 + b0
            left[A_ROWS * r : A_ROWS * (r + 1), t * LANES : (t + 1) * LANES] = a_refs[flip][piece]
            tail.append(a_refs[flip][piece, A_ROWS - 16 :, :].astype(jnp.float32)[8:])
        tails.append(jnp.concatenate(tail, axis=0))
        for c in range(4):
            columns = slice(c * LANES, (c + 1) * LANES)
            piece = 4 * (2 * b1 + b0) + c
            right[t * LANES : (t + 1) * LANES, columns] = b_ref[2 * b3 + b2, piece, 0:LANES, :]
            right[MAIN + t * REST : MAIN + (t + 1) * REST, columns] = b_ref[2 * b3 + b2, piece, LANES:, :]
    spread[...] = jnp.zeros_like(spread)
    for half in range(2):
        for g in range(ROWS // 8):
            rest = jnp.zeros((4 * 8, LANES), jnp.float32)
            for place in range(8):
                shift = REST * (place - g) % LANES
                tile = tails[8 * half + place]
                moved = pltpu.roll(tile, shift, 1) if shift else tile
                rest = jnp.where(lane_group == place, moved, rest)
            for r in range(4):
                spread[A_ROWS * r + 8 * g : A_ROWS * r + 8 * g + 8, half * LANES : (half + 1) * LANES] = rest[8 * r : 8 * r + 8]
    left[:, MAIN:] = spread[...].astype(jnp.bfloat16)
    total = jnp.dot(left[...], right[...], preferred_element_type=jnp.float32)
    for r in range(4):
        for c in range(4):
            out_ref[4 * r + c] = total[A_ROWS * r : A_ROWS * r + ROWS, c * LANES : (c + 1) * LANES]


def multiply(my_zh, a_slots, b_slots):
    depth = PIECES * (LANES + REST)
    return pl.pallas_call(
        multiply_kernel,
        out_shape=jax.ShapeDtypeStruct((PIECES, ROWS, LANES), jnp.float32),
        in_specs=[pl.BlockSpec(memory_space=pltpu.SMEM)] + [pl.BlockSpec(memory_space=pltpu.VMEM)] * 5,
        out_specs=pl.BlockSpec(memory_space=pltpu.VMEM),
        scratch_shapes=[
            pltpu.VMEM((4 * A_ROWS, depth), jnp.bfloat16),
            pltpu.VMEM((depth, 4 * LANES), jnp.bfloat16),
            pltpu.VMEM((4 * A_ROWS, 2 * LANES), jnp.float32),
        ],
        compiler_params=pltpu.CompilerParams(vmem_limit_bytes=VMEM),
    )(my_zh, *a_slots, b_slots)


def body(amplitudes, integrals, other_terms, occ_energy, virt_energy):
    pieces = lax.all_to_all(pack(amplitudes, integrals), NEAR, 0, 0, tiled=True)
    a, b = pieces[:, :A_ROWS], pieces[:, A_ROWS:]
    a_slots = [a] + [lax.ppermute(a, "zh", [(i, i ^ d) for i in range(4)]) for d in (1, 2, 3)]
    b_slots = lax.all_to_all(jnp.broadcast_to(b[None], (4,) + b.shape), "yh", 0, 0, tiled=True)
    my_zh = lax.axis_index("zh").astype(jnp.int32)[None]
    partial = multiply(my_zh, a_slots, b_slots)
    partial = lax.all_to_all(partial, NEAR, 0, 0, tiled=True)
    ladder = lax.psum(jnp.sum(partial, axis=0), "l")
    denominator = occ_energy[:, None] - virt_energy[None, :]
    return (ladder + other_terms) / denominator


def solution(mesh):
    fine = Mesh(mesh.devices.reshape(tuple(PARTS.values())), tuple(PARTS))
    row, col = ("yh", "yl", "xl"), ("xh", "zh", "zl")
    in_specs = (P(row, ("l",) + col), P(("l",) + row, col), P(row, col), P(row), P(col))
    return jax.shard_map(body, mesh=fine, in_specs=in_specs, out_specs=P(row, col), check_vma=False)
```

```python
import jax
import jax.numpy as jnp
from jax import lax
from jax.experimental import pallas as pl
from jax.experimental.pallas import tpu as pltpu
from jax.sharding import Mesh
from jax.sharding import PartitionSpec as P

PARTS = {"l": 2, "yh": 4, "yl": 2, "xl": 2, "xh": 2, "zh": 4, "zl": 2}
NEAR = ("yl", "xl", "xh", "zl")
PIECES = 16
ROWS = 56
LANES = 128
MAIN = PIECES * LANES
REST = 16
A_ROWS = 64
B_ROWS = LANES + REST
VMEM = 40 * 1024 * 1024


def pack_kernel(a_ref, b_ref, a_out, b_out):
    lane_group = lax.broadcasted_iota(jnp.int32, (8, LANES), 1) // REST
    tail = a_ref[:, MAIN:].astype(jnp.float32)
    for s in range(PIECES):
        main = a_ref[:, s * LANES : (s + 1) * LANES].astype(jnp.float32)
        half, place = divmod(s, 8)
        rest = jnp.zeros((8, LANES), jnp.float32)
        for g in range(ROWS // 8):
            tile = tail[8 * g : 8 * g + 8, half * LANES : (half + 1) * LANES]
            shift = REST * (g - place) % LANES
            moved = pltpu.roll(tile, shift, 1) if shift else tile
            rest = jnp.where(lane_group == g, moved, rest)
        a_out[s] = jnp.concatenate([main, rest], axis=0).astype(jnp.bfloat16)
        for far in range(4):
            b_out[far, s, 0:LANES, :] = b_ref[s * LANES : (s + 1) * LANES, :]
            b_out[far, s, LANES:, :] = b_ref[MAIN + s * REST : MAIN + (s + 1) * REST, :]


def pack(a, b):
    return pl.pallas_call(
        pack_kernel,
        out_shape=[
            jax.ShapeDtypeStruct((PIECES, A_ROWS, LANES), jnp.bfloat16),
            jax.ShapeDtypeStruct((4, PIECES, B_ROWS, LANES), jnp.bfloat16),
        ],
        in_specs=[pl.BlockSpec(memory_space=pltpu.VMEM)] * 2,
        out_specs=[pl.BlockSpec(memory_space=pltpu.VMEM)] * 2,
        compiler_params=pltpu.CompilerParams(vmem_limit_bytes=VMEM),
    )(a, b)


def multiply_kernel(my_zh_ref, *refs):
    a_refs, (b_ref, out_ref, left, right, spread) = refs[:4], refs[4:]
    my_zh = my_zh_ref[0]
    lane_group = lax.broadcasted_iota(jnp.int32, (4 * 8, LANES), 1) // REST
    tails = []
    for t in range(PIECES):
        flip, b3, b0 = t >> 2, (t >> 1) & 1, t & 1
        zh = my_zh ^ flip
        b2, b1 = zh >> 1, zh & 1
        tail = []
        for r in range(4):
            piece = 4 * r + 2 * b3 + b0
            left[A_ROWS * r : A_ROWS * (r + 1), t * LANES : (t + 1) * LANES] = a_refs[flip][piece]
            tail.append(a_refs[flip][piece, A_ROWS - 16 :, :].astype(jnp.float32)[8:])
        tails.append(jnp.concatenate(tail, axis=0))
        for c in range(4):
            columns = slice(c * LANES, (c + 1) * LANES)
            piece = 4 * (2 * b1 + b0) + c
            right[t * LANES : (t + 1) * LANES, columns] = b_ref[2 * b3 + b2, piece, 0:LANES, :]
            right[MAIN + t * REST : MAIN + (t + 1) * REST, columns] = b_ref[2 * b3 + b2, piece, LANES:, :]
    spread[...] = jnp.zeros_like(spread)
    for half in range(2):
        for g in range(ROWS // 8):
            rest = jnp.zeros((4 * 8, LANES), jnp.float32)
            for place in range(8):
                shift = REST * (place - g) % LANES
                tile = tails[8 * half + place]
                moved = pltpu.roll(tile, shift, 1) if shift else tile
                rest = jnp.where(lane_group == place, moved, rest)
            for r in range(4):
                spread[A_ROWS * r + 8 * g : A_ROWS * r + 8 * g + 8, half * LANES : (half + 1) * LANES] = rest[8 * r : 8 * r + 8]
    left[:, MAIN:] = spread[...].astype(jnp.bfloat16)
    total = jnp.dot(left[...], right[...], preferred_element_type=jnp.float32)
    for r in range(4):
        for c in range(4):
            out_ref[4 * r + c] = total[A_ROWS * r : A_ROWS * r + ROWS, c * LANES : (c + 1) * LANES]


def multiply(my_zh, a_slots, b_slots):
    depth = PIECES * (LANES + REST)
    return pl.pallas_call(
        multiply_kernel,
        out_shape=jax.ShapeDtypeStruct((PIECES, ROWS, LANES), jnp.float32),
        in_specs=[pl.BlockSpec(memory_space=pltpu.SMEM)] + [pl.BlockSpec(memory_space=pltpu.VMEM)] * 5,
        out_specs=pl.BlockSpec(memory_space=pltpu.VMEM),
        scratch_shapes=[
            pltpu.VMEM((4 * A_ROWS, depth), jnp.bfloat16),
            pltpu.VMEM((depth, 4 * LANES), jnp.bfloat16),
            pltpu.VMEM((4 * A_ROWS, 2 * LANES), jnp.float32),
        ],
        compiler_params=pltpu.CompilerParams(vmem_limit_bytes=VMEM),
    )(my_zh, *a_slots, b_slots)


def body(amplitudes, integrals, other_terms, occ_energy, virt_energy):
    a, b = pack(amplitudes, integrals)
    b_slots = lax.all_to_all(b.reshape((4 * PIECES,) + b.shape[2:]), ("yh",) + NEAR, 0, 0, tiled=True).reshape(b.shape)
    a = lax.all_to_all(a, NEAR, 0, 0, tiled=True)
    a_slots = [a] + [lax.ppermute(a, "zh", [(i, i ^ d) for i in range(4)]) for d in (1, 2, 3)]
    my_zh = lax.axis_index("zh").astype(jnp.int32)[None]
    partial = multiply(my_zh, a_slots, b_slots)
    partial = lax.all_to_all(partial, NEAR, 0, 0, tiled=True)
    ladder = lax.psum(jnp.sum(partial, axis=0), "l")
    denominator = occ_energy[:, None] - virt_energy[None, :]
    return (ladder + other_terms) / denominator


def solution(mesh):
    fine = Mesh(mesh.devices.reshape(tuple(PARTS.values())), tuple(PARTS))
    row, col = ("yh", "yl", "xl"), ("xh", "zh", "zl")
    in_specs = (P(row, ("l",) + col), P(("l",) + row, col), P(row, col), P(row), P(col))
    return jax.shard_map(body, mesh=fine, in_specs=in_specs, out_specs=P(row, col), check_vma=False)
```

```python
import jax
import jax.numpy as jnp
from jax import lax
from jax.experimental import pallas as pl
from jax.experimental.pallas import tpu as pltpu
from jax.sharding import Mesh
from jax.sharding import PartitionSpec as P

PARTS = {"l": 2, "y2": 2, "y1": 2, "yl": 2, "xl": 2, "xh": 2, "zh": 4, "zl": 2}
NEAR = ("yl", "xl", "xh", "zl")
PIECES = 32
BLOCKS = 16
ROWS = 56
LANES = 128
HALF = LANES // 2
REST = 8
MAIN = PIECES * HALF
GROUPS = ROWS // 8
B_ROWS = HALF + REST
R_BLOCKS = 8
C_BLOCKS = 4
A_ROWS = 64
VMEM = 40 * 1024 * 1024
f32, bf16 = jnp.float32, jnp.bfloat16


def rolled(x, shift):
    return pltpu.roll(x, shift % LANES, 1) if shift % LANES else x


def pack_kernel(a_ref, b_ref, a_out, b_out):
    lane = lax.broadcasted_iota(jnp.int32, (8, LANES), 1)
    left_half = lax.broadcasted_iota(jnp.int32, (24, LANES), 1) < HALF
    a_tail = a_ref[:, MAIN:].astype(f32)
    b_tail = b_ref[MAIN:, :].astype(f32)
    for s in range(PIECES):
        tile = a_ref[:, s // 2 * LANES : (s // 2 + 1) * LANES].astype(f32)
        upper, lower = rolled(tile[:32], s % 2 * HALF), rolled(tile[32:], (s + 1) % 2 * HALF)
        corner = upper[24:]
        for g in range(GROUPS):
            rest = a_tail[8 * g : 8 * g + 8, s // 16 * LANES : (s // 16 + 1) * LANES]
            rest = rolled(rest, HALF + REST * g - REST * (s % 16))
            corner = jnp.where((lane >= HALF) & (lane // REST == HALF // REST + g), rest, corner)
        piece = jnp.concatenate([jnp.where(left_half, upper[:24], lower), corner], axis=0)
        a_out[s] = piece.astype(bf16)
        piece = jnp.concatenate([b_ref[s * HALF : (s + 1) * HALF, :].astype(f32), b_tail[s * REST : (s + 1) * REST]], axis=0)
        for far in range(2):
            b_out[far * PIECES + s] = piece.astype(bf16)


def pack(a, b):
    return pl.pallas_call(
        pack_kernel,
        out_shape=[
            jax.ShapeDtypeStruct((PIECES, 32, LANES), bf16),
            jax.ShapeDtypeStruct((2 * PIECES, B_ROWS, LANES), bf16),
        ],
        in_specs=[pl.BlockSpec(memory_space=pltpu.VMEM)] * 2,
        out_specs=[pl.BlockSpec(memory_space=pltpu.VMEM)] * 2,
        compiler_params=pltpu.CompilerParams(vmem_limit_bytes=VMEM),
    )(a, b)


def multiply_kernel(my_zh_ref, *refs):
    a_refs, (b_ref, out_ref, left, right, spread) = refs[:4], refs[4:]
    my_zh = my_zh_ref[0]
    left_half = lax.broadcasted_iota(jnp.int32, (32, LANES), 1) < HALF
    lane_group = lax.broadcasted_iota(jnp.int32, (8 * R_BLOCKS, LANES), 1) // REST
    main = BLOCKS * HALF
    corners = []
    b_rest = [[] for _ in range(C_BLOCKS)]
    for pair in range(BLOCKS // 2):
        flip, b3 = pair >> 1, pair & 1
        columns = slice(pair * LANES, (pair + 1) * LANES)
        corner = [[], []]
        for r in range(R_BLOCKS):
            p0 = a_refs[flip][4 * r + 2 * b3].astype(f32)
            p1 = a_refs[flip][4 * r + 2 * b3 + 1].astype(f32)
            upper = jnp.where(left_half, p0, rolled(p1, HALF))
            lower = jnp.where(left_half, rolled(p0, HALF), p1)
            left[A_ROWS * r : A_ROWS * r + 32, columns] = upper.astype(bf16)
            left[A_ROWS * r + 32 : A_ROWS * (r + 1), columns] = lower.astype(bf16)
            corner[0].append(p0[24:])
            corner[1].append(p1[24:])
        corners += [jnp.concatenate(c, axis=0) for c in corner]
        for b0 in range(2):
            block = 8 * b3 + 2 * (my_zh ^ flip) + b0
            at = (2 * pair + b0) * HALF
            for c in range(C_BLOCKS):
                piece = b_ref[C_BLOCKS * block + c]
                right[at : at + HALF, c * LANES : (c + 1) * LANES] = piece[:HALF]
                b_rest[c].append(piece.astype(f32)[HALF:])
    for c in range(C_BLOCKS):
        right[main:, c * LANES : (c + 1) * LANES] = jnp.concatenate(b_rest[c], axis=0).astype(bf16)
    for g in range(8):
        rest = jnp.zeros((8 * R_BLOCKS, LANES), f32)
        for t in range(BLOCKS if g < GROUPS else 0):
            rest = jnp.where(lane_group == t, rolled(corners[t], REST * (t - g) - HALF), rest)
        for r in range(R_BLOCKS):
            spread[A_ROWS * r + 8 * g : A_ROWS * r + 8 * g + 8, :] = rest[8 * r : 8 * r + 8]
    left[:, main:] = spread[...].astype(bf16)
    for r in range(R_BLOCKS):
        y1, near_row = divmod(r, 4)
        if r % 4 == 0:
            total = jnp.dot(left[A_ROWS * r : A_ROWS * (r + 4), :], right[...], preferred_element_type=f32)
        for c in range(C_BLOCKS):
            out_ref[C_BLOCKS * near_row + c, y1] = total[A_ROWS * near_row : A_ROWS * near_row + ROWS, c * LANES : (c + 1) * LANES]


def multiply(my_zh, a_slots, b_slots):
    depth = BLOCKS * B_ROWS
    return pl.pallas_call(
        multiply_kernel,
        out_shape=jax.ShapeDtypeStruct((16, 2, ROWS, LANES), f32),
        in_specs=[pl.BlockSpec(memory_space=pltpu.SMEM)] + [pl.BlockSpec(memory_space=pltpu.VMEM)] * 5,
        out_specs=pl.BlockSpec(memory_space=pltpu.VMEM),
        scratch_shapes=[
            pltpu.VMEM((R_BLOCKS * A_ROWS, depth), bf16),
            pltpu.VMEM((depth, C_BLOCKS * LANES), bf16),
            pltpu.VMEM((R_BLOCKS * A_ROWS, LANES), f32),
        ],
        compiler_params=pltpu.CompilerParams(vmem_limit_bytes=VMEM),
    )(my_zh, *a_slots, b_slots)


def body(amplitudes, integrals, other_terms, occ_energy, virt_energy):
    a, b = pack(amplitudes, integrals)
    b_slots = lax.all_to_all(b, ("y2", "y1") + NEAR, 0, 0, tiled=True)
    a = lax.all_to_all(a, ("y1",) + NEAR, 0, 0, tiled=True)
    a_slots = [a] + [lax.ppermute(a, "zh", [(i, i ^ d) for i in range(4)]) for d in (1, 2, 3)]
    my_zh = lax.axis_index("zh").astype(jnp.int32)[None]
    tiles = lax.all_to_all(multiply(my_zh, a_slots, b_slots), NEAR, 0, 0, tiled=True)
    tiles = jnp.sum(tiles, axis=0)
    tiles = lax.all_to_all(jnp.concatenate([tiles, tiles]), ("l", "y1"), 0, 0, tiled=True)
    denominator = occ_energy[:, None] - virt_energy[None, :]
    return (jnp.sum(tiles, axis=0) + other_terms) / denominator


def solution(mesh):
    fine = Mesh(mesh.devices.reshape(tuple(PARTS.values())), tuple(PARTS))
    row, col = ("y2", "y1", "yl", "xl"), ("xh", "zh", "zl")
    in_specs = (P(row, ("l",) + col), P(("l",) + row, col), P(row, col), P(row), P(col))
    return jax.shard_map(body, mesh=fine, in_specs=in_specs, out_specs=P(row, col), check_vma=False)
```

```python
import jax
import jax.numpy as jnp
from jax import lax
from jax.experimental import pallas as pl
from jax.experimental.pallas import tpu as pltpu
from jax.sharding import Mesh
from jax.sharding import PartitionSpec as P

PARTS = {"l": 2, "yh": 4, "yl": 2, "xl": 2, "xh": 2, "zh": 4, "zl": 2}
NEAR = ("yl", "xl", "xh", "zl")
PIECES = 16
ROWS = 56
LANES = 128
MAIN = PIECES * LANES
REST = 16
A_ROWS = 64
B_ROWS = LANES + REST
VMEM = 40 * 1024 * 1024


def pack_a_kernel(a_ref, out_ref):
    lane_group = lax.broadcasted_iota(jnp.int32, (8, LANES), 1) // REST
    tail = a_ref[:, MAIN:].astype(jnp.float32)
    for s in range(PIECES):
        main = a_ref[:, s * LANES : (s + 1) * LANES].astype(jnp.float32)
        half, place = divmod(s, 8)
        rest = jnp.zeros((8, LANES), jnp.float32)
        for g in range(ROWS // 8):
            tile = tail[8 * g : 8 * g + 8, half * LANES : (half + 1) * LANES]
            shift = REST * (g - place) % LANES
            moved = pltpu.roll(tile, shift, 1) if shift else tile
            rest = jnp.where(lane_group == g, moved, rest)
        out_ref[s] = jnp.concatenate([main, rest], axis=0).astype(jnp.bfloat16)


def pack_b_kernel(b_ref, out_ref):
    for s in range(PIECES):
        for far in range(4):
            out_ref[far, s, 0:LANES, :] = b_ref[s * LANES : (s + 1) * LANES, :]
            out_ref[far, s, LANES:, :] = b_ref[MAIN + s * REST : MAIN + (s + 1) * REST, :]


def pack(kernel, block, shape):
    return pl.pallas_call(
        kernel,
        out_shape=jax.ShapeDtypeStruct(shape, jnp.bfloat16),
        in_specs=[pl.BlockSpec(memory_space=pltpu.VMEM)],
        out_specs=pl.BlockSpec(memory_space=pltpu.VMEM),
        cost_estimate=pl.CostEstimate(flops=0, bytes_accessed=8 * block.size, transcendentals=0),
        compiler_params=pltpu.CompilerParams(vmem_limit_bytes=VMEM),
    )(block)


def multiply_kernel(my_zh_ref, *refs):
    a_refs, (b_ref, out_ref, left, right, spread) = refs[:4], refs[4:]
    my_zh = my_zh_ref[0]
    lane_group = lax.broadcasted_iota(jnp.int32, (4 * 8, LANES), 1) // REST
    tails = []
    for t in range(PIECES):
        flip, b3, b0 = t >> 2, (t >> 1) & 1, t & 1
        zh = my_zh ^ flip
        b2, b1 = zh >> 1, zh & 1
        tail = []
        for r in range(4):
            piece = 4 * r + 2 * b3 + b0
            left[A_ROWS * r : A_ROWS * (r + 1), t * LANES : (t + 1) * LANES] = a_refs[flip][piece]
            tail.append(a_refs[flip][piece, A_ROWS - 16 :, :].astype(jnp.float32)[8:])
        tails.append(jnp.concatenate(tail, axis=0))
        for c in range(4):
            columns = slice(c * LANES, (c + 1) * LANES)
            piece = 4 * (2 * b1 + b0) + c
            right[t * LANES : (t + 1) * LANES, columns] = b_ref[2 * b3 + b2, piece, 0:LANES, :]
            right[MAIN + t * REST : MAIN + (t + 1) * REST, columns] = b_ref[2 * b3 + b2, piece, LANES:, :]
    spread[...] = jnp.zeros_like(spread)
    for half in range(2):
        for g in range(ROWS // 8):
            rest = jnp.zeros((4 * 8, LANES), jnp.float32)
            for place in range(8):
                shift = REST * (place - g) % LANES
                tile = tails[8 * half + place]
                moved = pltpu.roll(tile, shift, 1) if shift else tile
                rest = jnp.where(lane_group == place, moved, rest)
            for r in range(4):
                spread[A_ROWS * r + 8 * g : A_ROWS * r + 8 * g + 8, half * LANES : (half + 1) * LANES] = rest[8 * r : 8 * r + 8]
    left[:, MAIN:] = spread[...].astype(jnp.bfloat16)
    total = jnp.dot(left[...], right[...], preferred_element_type=jnp.float32)
    for r in range(4):
        for c in range(4):
            out_ref[4 * r + c] = total[A_ROWS * r : A_ROWS * r + ROWS, c * LANES : (c + 1) * LANES]


def multiply(my_zh, a_slots, b_slots):
    depth = PIECES * (LANES + REST)
    return pl.pallas_call(
        multiply_kernel,
        out_shape=jax.ShapeDtypeStruct((PIECES, ROWS, LANES), jnp.float32),
        in_specs=[pl.BlockSpec(memory_space=pltpu.SMEM)] + [pl.BlockSpec(memory_space=pltpu.VMEM)] * 5,
        out_specs=pl.BlockSpec(memory_space=pltpu.VMEM),
        scratch_shapes=[
            pltpu.VMEM((4 * A_ROWS, depth), jnp.bfloat16),
            pltpu.VMEM((depth, 4 * LANES), jnp.bfloat16),
            pltpu.VMEM((4 * A_ROWS, 2 * LANES), jnp.float32),
        ],
        compiler_params=pltpu.CompilerParams(vmem_limit_bytes=VMEM),
    )(my_zh, *a_slots, b_slots)


def body(amplitudes, integrals, other_terms, occ_energy, virt_energy):
    a = pack(pack_a_kernel, amplitudes, (PIECES, A_ROWS, LANES))
    b = pack(pack_b_kernel, integrals, (4, PIECES, B_ROWS, LANES))
    b_slots = lax.all_to_all(b.reshape((4 * PIECES,) + b.shape[2:]), ("yh",) + NEAR, 0, 0, tiled=True).reshape(b.shape)
    a = lax.all_to_all(a, NEAR, 0, 0, tiled=True)
    a_slots = [a] + [lax.ppermute(a, "zh", [(i, i ^ d) for i in range(4)]) for d in (1, 2, 3)]
    my_zh = lax.axis_index("zh").astype(jnp.int32)[None]
    partial = multiply(my_zh, a_slots, b_slots)
    partial = lax.all_to_all(partial, NEAR, 0, 0, tiled=True)
    ladder = lax.psum(jnp.sum(partial, axis=0), "l")
    denominator = occ_energy[:, None] - virt_energy[None, :]
    return (ladder + other_terms) / denominator


def solution(mesh):
    fine = Mesh(mesh.devices.reshape(tuple(PARTS.values())), tuple(PARTS))
    row, col = ("yh", "yl", "xl"), ("xh", "zh", "zl")
    in_specs = (P(row, ("l",) + col), P(("l",) + row, col), P(row, col), P(row), P(col))
    return jax.shard_map(body, mesh=fine, in_specs=in_specs, out_specs=P(row, col), check_vma=False)
```

```python
import jax
import jax.numpy as jnp
from jax import lax
from jax.experimental import pallas as pl
from jax.experimental.pallas import tpu as pltpu
from jax.sharding import Mesh
from jax.sharding import PartitionSpec as P

PARTS = {"l": 2, "yh": 4, "yl": 2, "xl": 2, "xh": 2, "zh": 4, "zl": 2}
NEAR = ("yl", "xl", "xh")
PIECES = 8
BLOCKS = 16
ROWS = 56
LANES = 128
WIDE = 2 * LANES
REST = 32
MAIN = PIECES * WIDE
GROUPS = ROWS // 8
PLACES = LANES // REST
A_ROWS = 128
B_ROWS = WIDE + REST
R_ROWS = 64
VMEM = 40 * 1024 * 1024
f32, bf16 = jnp.float32, jnp.bfloat16


def rolled(x, shift):
    return pltpu.roll(x, shift % LANES, 1) if shift % LANES else x


def pack_a_kernel(a_ref, out_ref):
    lane_group = lax.broadcasted_iota(jnp.int32, (8, LANES), 1) // REST
    tail = a_ref[:, MAIN:].astype(f32)
    for s in range(PIECES):
        parts = [a_ref[:, (2 * s + i) * LANES : (2 * s + i + 1) * LANES].astype(f32) for i in range(2)]
        half, place = divmod(s, PLACES)
        rest = [jnp.zeros((8, LANES), f32)] * 2
        for g in range(GROUPS):
            q, u = divmod(g, PLACES)
            tile = tail[8 * g : 8 * g + 8, half * LANES : (half + 1) * LANES]
            rest[q] = jnp.where(lane_group == u, rolled(tile, REST * (u - place)), rest[q])
        piece = jnp.concatenate(parts + rest, axis=0).astype(bf16)
        for zl in range(2):
            out_ref[2 * s + zl] = piece


def pack_b_kernel(b_ref, out_ref):
    for s in range(PIECES):
        for far in range(4):
            out_ref[far * PIECES + s, 0:WIDE, :] = b_ref[s * WIDE : (s + 1) * WIDE, :]
            out_ref[far * PIECES + s, WIDE:, :] = b_ref[MAIN + s * REST : MAIN + (s + 1) * REST, :]


def pack(kernel, block, shape):
    return pl.pallas_call(
        kernel,
        out_shape=jax.ShapeDtypeStruct(shape, bf16),
        in_specs=[pl.BlockSpec(memory_space=pltpu.VMEM)],
        out_specs=pl.BlockSpec(memory_space=pltpu.VMEM),
        cost_estimate=pl.CostEstimate(flops=0, bytes_accessed=8 * block.size, transcendentals=0),
        compiler_params=pltpu.CompilerParams(vmem_limit_bytes=VMEM),
    )(block)


def multiply_kernel(my_zh_ref, *refs):
    a_refs, (b_ref, out_ref, left, right, spread) = refs[:4], refs[4:]
    my_zh = my_zh_ref[0]
    lane_group = lax.broadcasted_iota(jnp.int32, (4 * 8, LANES), 1) // REST
    main = BLOCKS * WIDE
    corners = []
    for t in range(BLOCKS):
        flip, b3, b0 = t >> 2, (t >> 1) & 1, t & 1
        block = 8 * b3 + 2 * (my_zh ^ flip) + b0
        corner = [[], []]
        for r in range(4):
            piece = a_refs[flip][4 * r + 2 * b3 + b0]
            wide = piece.astype(f32)
            rows = slice(R_ROWS * r, R_ROWS * (r + 1))
            left[rows, t * WIDE : t * WIDE + LANES] = piece[:R_ROWS]
            left[rows, t * WIDE + LANES : (t + 1) * WIDE] = wide[ROWS : ROWS + R_ROWS].astype(bf16)
            corner[0].append(wide[2 * ROWS : 2 * ROWS + 8])
            corner[1].append(wide[2 * ROWS + 8 :])
        corners.append([jnp.concatenate(c, axis=0) for c in corner])
        for c in range(2):
            columns = slice(c * LANES, (c + 1) * LANES)
            right[t * WIDE : (t + 1) * WIDE, columns] = b_ref[2 * block + c, 0:WIDE, :]
            right[main + t * REST : main + (t + 1) * REST, columns] = b_ref[2 * block + c, WIDE:, :]
    spread[...] = jnp.zeros_like(spread)
    for tile in range(BLOCKS // PLACES):
        for g in range(GROUPS):
            q, u = divmod(g, PLACES)
            rest = jnp.zeros((4 * 8, LANES), f32)
            for place in range(PLACES):
                moved = rolled(corners[PLACES * tile + place][q], REST * (place - u))
                rest = jnp.where(lane_group == place, moved, rest)
            for r in range(4):
                spread[R_ROWS * r + 8 * g : R_ROWS * r + 8 * g + 8, tile * LANES : (tile + 1) * LANES] = rest[8 * r : 8 * r + 8]
    left[:, main:] = spread[...].astype(bf16)
    total = jnp.dot(left[...], right[...], preferred_element_type=f32)
    for r in range(4):
        for c in range(2):
            out_ref[2 * r + c] = total[R_ROWS * r : R_ROWS * r + ROWS, c * LANES : (c + 1) * LANES]


def multiply(my_zh, a_slots, b_slots):
    depth = BLOCKS * B_ROWS
    return pl.pallas_call(
        multiply_kernel,
        out_shape=jax.ShapeDtypeStruct((PIECES, ROWS, LANES), f32),
        in_specs=[pl.BlockSpec(memory_space=pltpu.SMEM)] + [pl.BlockSpec(memory_space=pltpu.VMEM)] * 5,
        out_specs=pl.BlockSpec(memory_space=pltpu.VMEM),
        scratch_shapes=[
            pltpu.VMEM((4 * R_ROWS, depth), bf16),
            pltpu.VMEM((depth, 2 * LANES), bf16),
            pltpu.VMEM((4 * R_ROWS, BLOCKS * REST), f32),
        ],
        compiler_params=pltpu.CompilerParams(vmem_limit_bytes=VMEM),
    )(my_zh, *a_slots, b_slots)


def body(amplitudes, integrals, other_terms, occ_energy, virt_energy):
    a = pack(pack_a_kernel, amplitudes, (2 * PIECES, A_ROWS, LANES))
    b = pack(pack_b_kernel, integrals, (4 * PIECES, B_ROWS, LANES))
    b_slots = lax.all_to_all(b, ("yh",) + NEAR, 0, 0, tiled=True)
    a = lax.all_to_all(a, NEAR + ("zl",), 0, 0, tiled=True)
    a_slots = [a] + [lax.ppermute(a, "zh", [(i, i ^ d) for i in range(4)]) for d in (1, 2, 3)]
    my_zh = lax.axis_index("zh").astype(jnp.int32)[None]
    partial = multiply(my_zh, a_slots, b_slots)
    partial = lax.all_to_all(partial, NEAR, 0, 0, tiled=True)
    ladder = lax.psum(jnp.sum(partial, axis=0), "l")
    denominator = occ_energy[:, None] - virt_energy[None, :]
    return (ladder + other_terms) / denominator


def solution(mesh):
    fine = Mesh(mesh.devices.reshape(tuple(PARTS.values())), tuple(PARTS))
    row, col = ("yh", "yl", "xl"), ("xh", "zh", "zl")
    in_specs = (P(row, ("l",) + col), P(("l",) + row, col), P(row, col), P(row), P(col))
    return jax.shard_map(body, mesh=fine, in_specs=in_specs, out_specs=P(row, col), check_vma=False)
```

```python
import jax
import jax.numpy as jnp
from jax import lax
from jax.experimental import pallas as pl
from jax.experimental.pallas import tpu as pltpu
from jax.sharding import Mesh
from jax.sharding import PartitionSpec as P

PARTS = {"l": 2, "yh": 4, "yl": 2, "xl": 2, "xh": 2, "zh": 4, "zl": 2}
NEAR = ("yl", "xl", "xh", "zl")
PIECES = 16
ROWS = 56
LANES = 128
MAIN = PIECES * LANES
REST = 16
A_ROWS = 64
B_ROWS = LANES + REST
VMEM = 40 * 1024 * 1024


def pack_a_kernel(a_ref, out_ref):
    lane_group = lax.broadcasted_iota(jnp.int32, (8, LANES), 1) // REST
    tail = a_ref[:, MAIN:].astype(jnp.float32)
    for s in range(PIECES):
        main = a_ref[:, s * LANES : (s + 1) * LANES].astype(jnp.float32)
        half, place = divmod(s, 8)
        rest = jnp.zeros((8, LANES), jnp.float32)
        for g in range(ROWS // 8):
            tile = tail[8 * g : 8 * g + 8, half * LANES : (half + 1) * LANES]
            shift = REST * (g - place) % LANES
            moved = pltpu.roll(tile, shift, 1) if shift else tile
            rest = jnp.where(lane_group == g, moved, rest)
        out_ref[s] = jnp.concatenate([main, rest], axis=0).astype(jnp.bfloat16)


def pack_b_kernel(b_ref, out_ref):
    for s in range(PIECES):
        for far in range(4):
            out_ref[s, far, 0:LANES, :] = b_ref[s * LANES : (s + 1) * LANES, :]
            out_ref[s, far, LANES:, :] = b_ref[MAIN + s * REST : MAIN + (s + 1) * REST, :]


def pack(kernel, block, shape):
    return pl.pallas_call(
        kernel,
        out_shape=jax.ShapeDtypeStruct(shape, jnp.bfloat16),
        in_specs=[pl.BlockSpec(memory_space=pltpu.VMEM)],
        out_specs=pl.BlockSpec(memory_space=pltpu.VMEM),
        cost_estimate=pl.CostEstimate(flops=0, bytes_accessed=8 * block.size, transcendentals=0),
        compiler_params=pltpu.CompilerParams(vmem_limit_bytes=VMEM),
    )(block)


def multiply_kernel(my_zh_ref, *refs):
    a_refs, (b_ref, out_ref, left, right, spread) = refs[:4], refs[4:]
    my_zh = my_zh_ref[0]
    lane_group = lax.broadcasted_iota(jnp.int32, (4 * 8, LANES), 1) // REST
    tails = []
    for t in range(PIECES):
        flip, b3, b0 = t >> 2, (t >> 1) & 1, t & 1
        zh = my_zh ^ flip
        b2, b1 = zh >> 1, zh & 1
        tail = []
        for r in range(4):
            piece = 4 * r + 2 * b3 + b0
            left[A_ROWS * r : A_ROWS * (r + 1), t * LANES : (t + 1) * LANES] = a_refs[flip][piece]
            tail.append(a_refs[flip][piece, A_ROWS - 16 :, :].astype(jnp.float32)[8:])
        tails.append(jnp.concatenate(tail, axis=0))
        for c in range(4):
            columns = slice(c * LANES, (c + 1) * LANES)
            piece = 4 * (2 * b1 + b0) + c
            right[t * LANES : (t + 1) * LANES, columns] = b_ref[piece, 2 * b3 + b2, 0:LANES, :]
            right[MAIN + t * REST : MAIN + (t + 1) * REST, columns] = b_ref[piece, 2 * b3 + b2, LANES:, :]
    spread[...] = jnp.zeros_like(spread)
    for half in range(2):
        for g in range(ROWS // 8):
            rest = jnp.zeros((4 * 8, LANES), jnp.float32)
            for place in range(8):
                shift = REST * (place - g) % LANES
                tile = tails[8 * half + place]
                moved = pltpu.roll(tile, shift, 1) if shift else tile
                rest = jnp.where(lane_group == place, moved, rest)
            for r in range(4):
                spread[A_ROWS * r + 8 * g : A_ROWS * r + 8 * g + 8, half * LANES : (half + 1) * LANES] = rest[8 * r : 8 * r + 8]
    left[:, MAIN:] = spread[...].astype(jnp.bfloat16)
    total = jnp.dot(left[...], right[...], preferred_element_type=jnp.float32)
    for r in range(4):
        for c in range(4):
            out_ref[4 * r + c] = total[A_ROWS * r : A_ROWS * r + ROWS, c * LANES : (c + 1) * LANES]


def multiply(my_zh, a_slots, b_slots):
    depth = PIECES * (LANES + REST)
    return pl.pallas_call(
        multiply_kernel,
        out_shape=jax.ShapeDtypeStruct((PIECES, ROWS, LANES), jnp.float32),
        in_specs=[pl.BlockSpec(memory_space=pltpu.SMEM)] + [pl.BlockSpec(memory_space=pltpu.VMEM)] * 5,
        out_specs=pl.BlockSpec(memory_space=pltpu.VMEM),
        scratch_shapes=[
            pltpu.VMEM((4 * A_ROWS, depth), jnp.bfloat16),
            pltpu.VMEM((depth, 4 * LANES), jnp.bfloat16),
            pltpu.VMEM((4 * A_ROWS, 2 * LANES), jnp.float32),
        ],
        compiler_params=pltpu.CompilerParams(vmem_limit_bytes=VMEM),
    )(my_zh, *a_slots, b_slots)


def body(amplitudes, integrals, other_terms, occ_energy, virt_energy):
    a = pack(pack_a_kernel, amplitudes, (PIECES, A_ROWS, LANES))
    b = pack(pack_b_kernel, integrals, (PIECES, 4, B_ROWS, LANES))
    b_slots = lax.all_to_all(b.reshape((4 * PIECES,) + b.shape[2:]), NEAR + ("yh",), 0, 0, tiled=True).reshape(b.shape)
    a = lax.all_to_all(a, NEAR, 0, 0, tiled=True)
    a_slots = [a] + [lax.ppermute(a, "zh", [(i, i ^ d) for i in range(4)]) for d in (1, 2, 3)]
    my_zh = lax.axis_index("zh").astype(jnp.int32)[None]
    partial = multiply(my_zh, a_slots, b_slots)
    partial = lax.all_to_all(partial, NEAR, 0, 0, tiled=True)
    ladder = lax.psum(jnp.sum(partial, axis=0), "l")
    denominator = occ_energy[:, None] - virt_energy[None, :]
    return (ladder + other_terms) / denominator


def solution(mesh):
    fine = Mesh(mesh.devices.reshape(tuple(PARTS.values())), tuple(PARTS))
    row, col = ("yh", "yl", "xl"), ("xh", "zh", "zl")
    in_specs = (P(row, ("l",) + col), P(("l",) + row, col), P(row, col), P(row), P(col))
    return jax.shard_map(body, mesh=fine, in_specs=in_specs, out_specs=P(row, col), check_vma=False)
```

```python
import jax
import jax.numpy as jnp
from jax import lax
from jax.experimental import pallas as pl
from jax.experimental.pallas import tpu as pltpu
from jax.sharding import Mesh
from jax.sharding import PartitionSpec as P

PARTS = {"l": 2, "yh": 4, "yl": 2, "xl": 2, "xh": 2, "zh": 4, "zl": 2}
NEAR = ("yl", "xl", "xh", "zl")
PIECES = 16
ROWS = 56
LANES = 128
MAIN = PIECES * LANES
REST = 16
A_ROWS = 64
B_ROWS = LANES + REST
VMEM = 40 * 1024 * 1024


def pack_a_kernel(a_ref, out_ref):
    lane_group = lax.broadcasted_iota(jnp.int32, (8, LANES), 1) // REST
    tail = a_ref[:, MAIN:].astype(jnp.float32)
    for s in range(PIECES):
        main = a_ref[:, s * LANES : (s + 1) * LANES].astype(jnp.float32)
        half, place = divmod(s, 8)
        rest = jnp.zeros((8, LANES), jnp.float32)
        for g in range(ROWS // 8):
            tile = tail[8 * g : 8 * g + 8, half * LANES : (half + 1) * LANES]
            shift = REST * (g - place) % LANES
            moved = pltpu.roll(tile, shift, 1) if shift else tile
            rest = jnp.where(lane_group == g, moved, rest)
        out_ref[s] = jnp.concatenate([main, rest], axis=0).astype(jnp.bfloat16)


def pack_b_kernel(b_ref, out_ref):
    for s in range(PIECES):
        for far in range(4):
            out_ref[s, far, 0:LANES, :] = b_ref[s * LANES : (s + 1) * LANES, :]
            out_ref[s, far, LANES:, :] = b_ref[MAIN + s * REST : MAIN + (s + 1) * REST, :]


def pack(kernel, block, shape):
    return pl.pallas_call(
        kernel,
        out_shape=jax.ShapeDtypeStruct(shape, jnp.bfloat16),
        in_specs=[pl.BlockSpec(memory_space=pltpu.VMEM)],
        out_specs=pl.BlockSpec(memory_space=pltpu.VMEM),
        cost_estimate=pl.CostEstimate(flops=0, bytes_accessed=8 * block.size, transcendentals=0),
        compiler_params=pltpu.CompilerParams(vmem_limit_bytes=VMEM),
    )(block)


def multiply_kernel(my_zh_ref, *refs):
    a_refs, (b_ref, out_ref, left, right, spread) = refs[:4], refs[4:]
    my_zh = my_zh_ref[0]
    lane_group = lax.broadcasted_iota(jnp.int32, (4 * 8, LANES), 1) // REST
    tails = []
    for t in range(PIECES):
        flip, b3, b0 = t >> 2, (t >> 1) & 1, t & 1
        zh = my_zh ^ flip
        b2, b1 = zh >> 1, zh & 1
        tail = []
        for r in range(4):
            piece = 4 * r + 2 * b3 + b0
            left[A_ROWS * r : A_ROWS * (r + 1), t * LANES : (t + 1) * LANES] = a_refs[flip][piece]
            tail.append(a_refs[flip][piece, A_ROWS - 16 :, :].astype(jnp.float32)[8:])
        tails.append(jnp.concatenate(tail, axis=0))
        for c in range(4):
            columns = slice(c * LANES, (c + 1) * LANES)
            piece = 4 * (2 * b1 + b0) + c
            right[t * LANES : (t + 1) * LANES, columns] = b_ref[piece, 2 * b3 + b2, 0:LANES, :]
            right[MAIN + t * REST : MAIN + (t + 1) * REST, columns] = b_ref[piece, 2 * b3 + b2, LANES:, :]
    spread[...] = jnp.zeros_like(spread)
    for half in range(2):
        for g in range(ROWS // 8):
            rest = jnp.zeros((4 * 8, LANES), jnp.float32)
            for place in range(8):
                shift = REST * (place - g) % LANES
                tile = tails[8 * half + place]
                moved = pltpu.roll(tile, shift, 1) if shift else tile
                rest = jnp.where(lane_group == place, moved, rest)
            for r in range(4):
                spread[A_ROWS * r + 8 * g : A_ROWS * r + 8 * g + 8, half * LANES : (half + 1) * LANES] = rest[8 * r : 8 * r + 8]
    left[:, MAIN:] = spread[...].astype(jnp.bfloat16)
    total = jnp.dot(left[...], right[...], preferred_element_type=jnp.float32)
    for r in range(4):
        for c in range(4):
            out_ref[4 * r + c] = total[A_ROWS * r : A_ROWS * r + ROWS, c * LANES : (c + 1) * LANES]


def multiply(my_zh, a_slots, b_slots):
    depth = PIECES * (LANES + REST)
    return pl.pallas_call(
        multiply_kernel,
        out_shape=jax.ShapeDtypeStruct((PIECES, ROWS, LANES), jnp.float32),
        in_specs=[pl.BlockSpec(memory_space=pltpu.SMEM)] + [pl.BlockSpec(memory_space=pltpu.VMEM)] * 5,
        out_specs=pl.BlockSpec(memory_space=pltpu.VMEM),
        scratch_shapes=[
            pltpu.VMEM((4 * A_ROWS, depth), jnp.bfloat16),
            pltpu.VMEM((depth, 4 * LANES), jnp.bfloat16),
            pltpu.VMEM((4 * A_ROWS, 2 * LANES), jnp.float32),
        ],
        compiler_params=pltpu.CompilerParams(vmem_limit_bytes=VMEM),
    )(my_zh, *a_slots, b_slots)


def body(amplitudes, integrals, other_terms, occ_energy, virt_energy):
    a = pack(pack_a_kernel, amplitudes, (PIECES, A_ROWS, LANES))
    b = pack(pack_b_kernel, integrals, (PIECES, 4, B_ROWS, LANES))
    b_slots = lax.all_to_all(b.reshape((4 * PIECES,) + b.shape[2:]), NEAR + ("yh",), 0, 0, tiled=True).reshape(b.shape)
    a = lax.all_to_all(a, NEAR, 0, 0, tiled=True)
    a_slots = [a] + [lax.ppermute(a, "zh", [(i, i ^ d) for i in range(4)]) for d in (1, 2, 3)]
    my_zh = lax.axis_index("zh").astype(jnp.int32)[None]
    partial = multiply(my_zh, a_slots, b_slots)
    partial = lax.all_to_all(partial, NEAR, 0, 0, tiled=True)
    mine = jnp.sum(partial, axis=0)
    ladder = mine + lax.ppermute(mine, "l", [(0, 1), (1, 0)])
    denominator = occ_energy[:, None] - virt_energy[None, :]
    return (ladder + other_terms) / denominator


def solution(mesh):
    fine = Mesh(mesh.devices.reshape(tuple(PARTS.values())), tuple(PARTS))
    row, col = ("yh", "yl", "xl"), ("xh", "zh", "zl")
    in_specs = (P(row, ("l",) + col), P(("l",) + row, col), P(row, col), P(row), P(col))
    return jax.shard_map(body, mesh=fine, in_specs=in_specs, out_specs=P(row, col), check_vma=False)
```

```python
import jax
import jax.numpy as jnp
from jax import lax
from jax.experimental import pallas as pl
from jax.experimental.pallas import tpu as pltpu
from jax.sharding import Mesh
from jax.sharding import PartitionSpec as P

PARTS = {"l": 2, "yh": 4, "yl": 2, "xl": 2, "xh": 2, "zh": 4, "zl": 2}
NEAR = ("yl", "xl", "xh", "zl")
PIECES = 16
ROWS = 56
LANES = 128
MAIN = PIECES * LANES
REST = 16
A_ROWS = 64
B_ROWS = LANES + REST
VMEM = 40 * 1024 * 1024


def pack_a_kernel(a_ref, b_tail_ref, out_ref):
    lane_group = lax.broadcasted_iota(jnp.int32, (8, LANES), 1) // REST
    tail = a_ref[:, MAIN:].astype(jnp.float32)
    for s in range(PIECES):
        main = a_ref[:, s * LANES : (s + 1) * LANES].astype(jnp.float32)
        half, place = divmod(s, 8)
        rest = jnp.zeros((8, LANES), jnp.float32)
        for g in range(ROWS // 8):
            tile = tail[8 * g : 8 * g + 8, half * LANES : (half + 1) * LANES]
            shift = REST * (g - place) % LANES
            moved = pltpu.roll(tile, shift, 1) if shift else tile
            rest = jnp.where(lane_group == g, moved, rest)
        out_ref[s, 0:A_ROWS, :] = jnp.concatenate([main, rest], axis=0).astype(jnp.bfloat16)
        out_ref[s, A_ROWS:, :] = b_tail_ref[s * REST : (s + 1) * REST, :]


def pack_a(a, b_tail):
    return pl.pallas_call(
        pack_a_kernel,
        out_shape=jax.ShapeDtypeStruct((PIECES, A_ROWS + REST, LANES), jnp.bfloat16),
        in_specs=[pl.BlockSpec(memory_space=pltpu.VMEM)] * 2,
        out_specs=pl.BlockSpec(memory_space=pltpu.VMEM),
        compiler_params=pltpu.CompilerParams(vmem_limit_bytes=VMEM),
    )(a, b_tail)


def pack_b_kernel(b_ref, out_ref):
    for s in range(PIECES):
        for far in range(4):
            out_ref[s, far] = b_ref[s * LANES : (s + 1) * LANES, :]


def pack_b(b):
    return pl.pallas_call(
        pack_b_kernel,
        out_shape=jax.ShapeDtypeStruct((PIECES, 4, LANES, LANES), jnp.bfloat16),
        in_specs=[pl.BlockSpec(memory_space=pltpu.VMEM)],
        out_specs=pl.BlockSpec(memory_space=pltpu.VMEM),
        cost_estimate=pl.CostEstimate(flops=0, bytes_accessed=8 * b.size, transcendentals=0),
        compiler_params=pltpu.CompilerParams(vmem_limit_bytes=VMEM),
    )(b)


def multiply_kernel(place_ref, *refs):
    a_refs, (b_ref, b_tail_ref, out_ref, left, right, spread) = refs[:4], refs[4:]
    my_zh, my_yh = place_ref[0], place_ref[1]
    lane_group = lax.broadcasted_iota(jnp.int32, (4 * 8, LANES), 1) // REST
    tails = []
    for t in range(PIECES):
        flip, b3, b0 = t >> 2, (t >> 1) & 1, t & 1
        zh = my_zh ^ flip
        b2, b1 = zh >> 1, zh & 1
        tail = []
        for r in range(4):
            piece = 4 * r + 2 * b3 + b0
            left[A_ROWS * r : A_ROWS * (r + 1), t * LANES : (t + 1) * LANES] = a_refs[flip][piece]
            tail.append(a_refs[flip][piece, A_ROWS - 16 :, :].astype(jnp.float32)[8:])
        tails.append(jnp.concatenate(tail, axis=0))
        for c in range(4):
            columns = slice(c * LANES, (c + 1) * LANES)
            piece = 4 * (2 * b1 + b0) + c
            right[t * LANES : (t + 1) * LANES, columns] = b_ref[piece, 2 * b3 + b2]
            right[MAIN + t * REST : MAIN + (t + 1) * REST, columns] = b_tail_ref[(2 * b3 + b2) ^ my_yh, piece]
    spread[...] = jnp.zeros_like(spread)
    for half in range(2):
        for g in range(ROWS // 8):
            rest = jnp.zeros((4 * 8, LANES), jnp.float32)
            for place in range(8):
                shift = REST * (place - g) % LANES
                tile = tails[8 * half + place]
                moved = pltpu.roll(tile, shift, 1) if shift else tile
                rest = jnp.where(lane_group == place, moved, rest)
            for r in range(4):
                spread[A_ROWS * r + 8 * g : A_ROWS * r + 8 * g + 8, half * LANES : (half + 1) * LANES] = rest[8 * r : 8 * r + 8]
    left[:, MAIN:] = spread[...].astype(jnp.bfloat16)
    total = jnp.dot(left[...], right[...], preferred_element_type=jnp.float32)
    for r in range(4):
        for c in range(4):
            out_ref[4 * r + c] = total[A_ROWS * r : A_ROWS * r + ROWS, c * LANES : (c + 1) * LANES]


def multiply(place, a_slots, b_slots, b_tails):
    depth = PIECES * (LANES + REST)
    return pl.pallas_call(
        multiply_kernel,
        out_shape=jax.ShapeDtypeStruct((PIECES, ROWS, LANES), jnp.float32),
        in_specs=[pl.BlockSpec(memory_space=pltpu.SMEM)] + [pl.BlockSpec(memory_space=pltpu.VMEM)] * 6,
        out_specs=pl.BlockSpec(memory_space=pltpu.VMEM),
        scratch_shapes=[
            pltpu.VMEM((4 * A_ROWS, depth), jnp.bfloat16),
            pltpu.VMEM((depth, 4 * LANES), jnp.bfloat16),
            pltpu.VMEM((4 * A_ROWS, 2 * LANES), jnp.float32),
        ],
        compiler_params=pltpu.CompilerParams(vmem_limit_bytes=VMEM),
    )(place, *a_slots, b_slots, b_tails)


def body(amplitudes, integrals, other_terms, occ_energy, virt_energy):
    near = lax.all_to_all(pack_a(amplitudes, integrals[MAIN:]), NEAR, 0, 0, tiled=True)
    a, b_tail = near[:, :A_ROWS], near[:, A_ROWS:]
    b = pack_b(integrals)
    b_slots = lax.all_to_all(b.reshape((4 * PIECES,) + b.shape[2:]), NEAR + ("yh",), 0, 0, tiled=True).reshape(b.shape)
    flips = [[(i, i ^ d) for i in range(4)] for d in (1, 2, 3)]
    b_tails = jnp.stack([b_tail] + [lax.ppermute(b_tail, "yh", flip) for flip in flips])
    a_slots = [a] + [lax.ppermute(a, "zh", flip) for flip in flips]
    place = jnp.stack([lax.axis_index("zh"), lax.axis_index("yh")]).astype(jnp.int32)
    partial = multiply(place, a_slots, b_slots, b_tails)
    partial = lax.all_to_all(partial, NEAR, 0, 0, tiled=True)
    mine = jnp.sum(partial, axis=0)
    ladder = mine + lax.ppermute(mine, "l", [(0, 1), (1, 0)])
    denominator = occ_energy[:, None] - virt_energy[None, :]
    return (ladder + other_terms) / denominator


def solution(mesh):
    fine = Mesh(mesh.devices.reshape(tuple(PARTS.values())), tuple(PARTS))
    row, col = ("yh", "yl", "xl"), ("xh", "zh", "zl")
    in_specs = (P(row, ("l",) + col), P(("l",) + row, col), P(row, col), P(row), P(col))
    return jax.shard_map(body, mesh=fine, in_specs=in_specs, out_specs=P(row, col), check_vma=False)
```

```python
import jax
import jax.numpy as jnp
from jax import lax
from jax.experimental import pallas as pl
from jax.experimental.pallas import tpu as pltpu
from jax.sharding import Mesh
from jax.sharding import PartitionSpec as P

PARTS = {"l": 2, "yh": 4, "yl": 2, "xl": 2, "xh": 2, "zh": 4, "zl": 2}
NEAR = ("yl", "xl", "xh", "zl")
PIECES = 16
ROWS = 56
LANES = 128
MAIN = PIECES * LANES
REST = 16
A_ROWS = 64
B_ROWS = LANES + REST
VMEM = 40 * 1024 * 1024


def pack_a_kernel(a_ref, out_ref):
    lane_group = lax.broadcasted_iota(jnp.int32, (8, LANES), 1) // REST
    tail = a_ref[:, MAIN:].astype(jnp.float32)
    for s in range(PIECES):
        main = a_ref[:, s * LANES : (s + 1) * LANES].astype(jnp.float32)
        half, place = divmod(s, 8)
        rest = jnp.zeros((8, LANES), jnp.float32)
        for g in range(ROWS // 8):
            tile = tail[8 * g : 8 * g + 8, half * LANES : (half + 1) * LANES]
            shift = REST * (g - place) % LANES
            moved = pltpu.roll(tile, shift, 1) if shift else tile
            rest = jnp.where(lane_group == g, moved, rest)
        out_ref[s] = jnp.concatenate([main, rest], axis=0).astype(jnp.bfloat16)


def pack_b_kernel(b_ref, out_ref):
    for s in range(PIECES):
        for far in range(4):
            out_ref[s, far, 0:LANES, :] = b_ref[s * LANES : (s + 1) * LANES, :]
            out_ref[s, far, LANES:, :] = b_ref[MAIN + s * REST : MAIN + (s + 1) * REST, :]


def pack(kernel, block, shape):
    return pl.pallas_call(
        kernel,
        out_shape=jax.ShapeDtypeStruct(shape, jnp.bfloat16),
        in_specs=[pl.BlockSpec(memory_space=pltpu.VMEM)],
        out_specs=pl.BlockSpec(memory_space=pltpu.VMEM),
        cost_estimate=pl.CostEstimate(flops=0, bytes_accessed=8 * block.size, transcendentals=0),
        compiler_params=pltpu.CompilerParams(vmem_limit_bytes=VMEM),
    )(block)


def multiply_kernel(my_zh_ref, *refs):
    a_refs, (b_ref, out_ref, left, right, spread) = refs[:4], refs[4:]
    my_zh = my_zh_ref[0]
    lane_group = lax.broadcasted_iota(jnp.int32, (4 * 8, LANES), 1) // REST
    tails = []
    for t in range(PIECES):
        flip, b3, b0 = t >> 2, (t >> 1) & 1, t & 1
        zh = my_zh ^ flip
        b2, b1 = zh >> 1, zh & 1
        tail = []
        for r in range(4):
            piece = 4 * r + 2 * b3 + b0
            left[A_ROWS * r : A_ROWS * (r + 1), t * LANES : (t + 1) * LANES] = a_refs[flip][piece]
            tail.append(a_refs[flip][piece, A_ROWS - 16 :, :].astype(jnp.float32)[8:])
        tails.append(jnp.concatenate(tail, axis=0))
        for c in range(4):
            columns = slice(c * LANES, (c + 1) * LANES)
            piece = 4 * (2 * b1 + b0) + c
            right[t * LANES : (t + 1) * LANES, columns] = b_ref[piece, 2 * b3 + b2, 0:LANES, :]
            right[MAIN + t * REST : MAIN + (t + 1) * REST, columns] = b_ref[piece, 2 * b3 + b2, LANES:, :]
        if t == PIECES // 2 - 1:
            part = slice(0, MAIN // 2)
            total = jnp.dot(left[:, part], right[part, :], preferred_element_type=jnp.float32)
    spread[...] = jnp.zeros_like(spread)
    for half in range(2):
        for g in range(ROWS // 8):
            rest = jnp.zeros((4 * 8, LANES), jnp.float32)
            for place in range(8):
                shift = REST * (place - g) % LANES
                tile = tails[8 * half + place]
                moved = pltpu.roll(tile, shift, 1) if shift else tile
                rest = jnp.where(lane_group == place, moved, rest)
            for r in range(4):
                spread[A_ROWS * r + 8 * g : A_ROWS * r + 8 * g + 8, half * LANES : (half + 1) * LANES] = rest[8 * r : 8 * r + 8]
    left[:, MAIN:] = spread[...].astype(jnp.bfloat16)
    part = slice(MAIN // 2, PIECES * (LANES + REST))
    total = total + jnp.dot(left[:, part], right[part, :], preferred_element_type=jnp.float32)
    for r in range(4):
        for c in range(4):
            out_ref[4 * r + c] = total[A_ROWS * r : A_ROWS * r + ROWS, c * LANES : (c + 1) * LANES]


def multiply(my_zh, a_slots, b_slots):
    depth = PIECES * (LANES + REST)
    return pl.pallas_call(
        multiply_kernel,
        out_shape=jax.ShapeDtypeStruct((PIECES, ROWS, LANES), jnp.float32),
        in_specs=[pl.BlockSpec(memory_space=pltpu.SMEM)] + [pl.BlockSpec(memory_space=pltpu.VMEM)] * 5,
        out_specs=pl.BlockSpec(memory_space=pltpu.VMEM),
        scratch_shapes=[
            pltpu.VMEM((4 * A_ROWS, depth), jnp.bfloat16),
            pltpu.VMEM((depth, 4 * LANES), jnp.bfloat16),
            pltpu.VMEM((4 * A_ROWS, 2 * LANES), jnp.float32),
        ],
        compiler_params=pltpu.CompilerParams(vmem_limit_bytes=VMEM),
    )(my_zh, *a_slots, b_slots)


def body(amplitudes, integrals, other_terms, occ_energy, virt_energy):
    a = pack(pack_a_kernel, amplitudes, (PIECES, A_ROWS, LANES))
    b = pack(pack_b_kernel, integrals, (PIECES, 4, B_ROWS, LANES))
    b_slots = lax.all_to_all(b.reshape((4 * PIECES,) + b.shape[2:]), NEAR + ("yh",), 0, 0, tiled=True).reshape(b.shape)
    a = lax.all_to_all(a, NEAR, 0, 0, tiled=True)
    a_slots = [a] + [lax.ppermute(a, "zh", [(i, i ^ d) for i in range(4)]) for d in (1, 2, 3)]
    my_zh = lax.axis_index("zh").astype(jnp.int32)[None]
    partial = multiply(my_zh, a_slots, b_slots)
    partial = lax.all_to_all(partial, NEAR, 0, 0, tiled=True)
    mine = jnp.sum(partial, axis=0)
    ladder = mine + lax.ppermute(mine, "l", [(0, 1), (1, 0)])
    denominator = occ_energy[:, None] - virt_energy[None, :]
    return (ladder + other_terms) / denominator


def solution(mesh):
    fine = Mesh(mesh.devices.reshape(tuple(PARTS.values())), tuple(PARTS))
    row, col = ("yh", "yl", "xl"), ("xh", "zh", "zl")
    in_specs = (P(row, ("l",) + col), P(("l",) + row, col), P(row, col), P(row), P(col))
    return jax.shard_map(body, mesh=fine, in_specs=in_specs, out_specs=P(row, col), check_vma=False)
```

```python
import jax
import jax.numpy as jnp
from jax import lax
from jax.experimental import pallas as pl
from jax.experimental.pallas import tpu as pltpu
from jax.sharding import Mesh
from jax.sharding import PartitionSpec as P

PARTS = {"l": 2, "yh": 4, "yl": 2, "xl": 2, "xh": 2, "zh": 4, "zl": 2}
NEAR = ("yl", "xl", "xh", "zl")
PIECES = 16
ROWS = 56
LANES = 128
MAIN = PIECES * LANES
REST = 16
A_ROWS = 64
B_ROWS = LANES + REST
VMEM = 40 * 1024 * 1024


def pack_a_kernel(a_ref, out_ref):
    lane_group = lax.broadcasted_iota(jnp.int32, (8, LANES), 1) // REST
    tail = a_ref[:, MAIN:].astype(jnp.float32)
    for s in range(PIECES):
        main = a_ref[:, s * LANES : (s + 1) * LANES].astype(jnp.float32)
        half, place = divmod(s, 8)
        rest = jnp.zeros((8, LANES), jnp.float32)
        for g in range(ROWS // 8):
            tile = tail[8 * g : 8 * g + 8, half * LANES : (half + 1) * LANES]
            shift = REST * (g - place) % LANES
            moved = pltpu.roll(tile, shift, 1) if shift else tile
            rest = jnp.where(lane_group == g, moved, rest)
        out_ref[s] = jnp.concatenate([main, rest], axis=0).astype(jnp.bfloat16)


def pack_b_kernel(b_ref, out_ref):
    for s in range(PIECES):
        for far in range(4):
            out_ref[s, far, 0:LANES, :] = b_ref[s * LANES : (s + 1) * LANES, :]
            out_ref[s, far, LANES:, :] = b_ref[MAIN + s * REST : MAIN + (s + 1) * REST, :]


def pack(kernel, block, shape):
    return pl.pallas_call(
        kernel,
        out_shape=jax.ShapeDtypeStruct(shape, jnp.bfloat16),
        in_specs=[pl.BlockSpec(memory_space=pltpu.VMEM)],
        out_specs=pl.BlockSpec(memory_space=pltpu.VMEM),
        cost_estimate=pl.CostEstimate(flops=0, bytes_accessed=8 * block.size, transcendentals=0),
        compiler_params=pltpu.CompilerParams(vmem_limit_bytes=VMEM),
    )(block)


def multiply_kernel(my_zh_ref, *refs):
    a_refs, (b_ref, out_ref, left, right, spread) = refs[:4], refs[4:]
    my_zh = my_zh_ref[0]
    lane_group = lax.broadcasted_iota(jnp.int32, (4 * 8, LANES), 1) // REST
    tails = []
    for t in range(PIECES):
        flip, b3, b0 = t >> 2, (t >> 1) & 1, t & 1
        zh = (my_zh + 4 - flip) & 3
        b2, b1 = zh >> 1, zh & 1
        tail = []
        for r in range(4):
            piece = 4 * r + 2 * b3 + b0
            left[A_ROWS * r : A_ROWS * (r + 1), t * LANES : (t + 1) * LANES] = a_refs[flip][piece]
            tail.append(a_refs[flip][piece, A_ROWS - 16 :, :].astype(jnp.float32)[8:])
        tails.append(jnp.concatenate(tail, axis=0))
        for c in range(4):
            columns = slice(c * LANES, (c + 1) * LANES)
            piece = 4 * (2 * b1 + b0) + c
            right[t * LANES : (t + 1) * LANES, columns] = b_ref[piece, 2 * b3 + b2, 0:LANES, :]
            right[MAIN + t * REST : MAIN + (t + 1) * REST, columns] = b_ref[piece, 2 * b3 + b2, LANES:, :]
    spread[...] = jnp.zeros_like(spread)
    for half in range(2):
        for g in range(ROWS // 8):
            rest = jnp.zeros((4 * 8, LANES), jnp.float32)
            for place in range(8):
                shift = REST * (place - g) % LANES
                tile = tails[8 * half + place]
                moved = pltpu.roll(tile, shift, 1) if shift else tile
                rest = jnp.where(lane_group == place, moved, rest)
            for r in range(4):
                spread[A_ROWS * r + 8 * g : A_ROWS * r + 8 * g + 8, half * LANES : (half + 1) * LANES] = rest[8 * r : 8 * r + 8]
    left[:, MAIN:] = spread[...].astype(jnp.bfloat16)
    total = jnp.dot(left[...], right[...], preferred_element_type=jnp.float32)
    for r in range(4):
        for c in range(4):
            out_ref[4 * r + c] = total[A_ROWS * r : A_ROWS * r + ROWS, c * LANES : (c + 1) * LANES]


def multiply(my_zh, a_slots, b_slots):
    depth = PIECES * (LANES + REST)
    return pl.pallas_call(
        multiply_kernel,
        out_shape=jax.ShapeDtypeStruct((PIECES, ROWS, LANES), jnp.float32),
        in_specs=[pl.BlockSpec(memory_space=pltpu.SMEM)] + [pl.BlockSpec(memory_space=pltpu.VMEM)] * 5,
        out_specs=pl.BlockSpec(memory_space=pltpu.VMEM),
        scratch_shapes=[
            pltpu.VMEM((4 * A_ROWS, depth), jnp.bfloat16),
            pltpu.VMEM((depth, 4 * LANES), jnp.bfloat16),
            pltpu.VMEM((4 * A_ROWS, 2 * LANES), jnp.float32),
        ],
        compiler_params=pltpu.CompilerParams(vmem_limit_bytes=VMEM),
    )(my_zh, *a_slots, b_slots)


def body(amplitudes, integrals, other_terms, occ_energy, virt_energy):
    a = pack(pack_a_kernel, amplitudes, (PIECES, A_ROWS, LANES))
    b = pack(pack_b_kernel, integrals, (PIECES, 4, B_ROWS, LANES))
    b_slots = lax.all_to_all(b.reshape((4 * PIECES,) + b.shape[2:]), NEAR + ("yh",), 0, 0, tiled=True).reshape(b.shape)
    a = lax.all_to_all(a, NEAR, 0, 0, tiled=True)
    a_slots = [a] + [lax.ppermute(a, "zh", [(i, (i + d) % 4) for i in range(4)]) for d in (1, 2, 3)]
    my_zh = lax.axis_index("zh").astype(jnp.int32)[None]
    partial = multiply(my_zh, a_slots, b_slots)
    partial = lax.all_to_all(partial, NEAR, 0, 0, tiled=True)
    mine = jnp.sum(partial, axis=0)
    ladder = mine + lax.ppermute(mine, "l", [(0, 1), (1, 0)])
    denominator = occ_energy[:, None] - virt_energy[None, :]
    return (ladder + other_terms) / denominator


def solution(mesh):
    fine = Mesh(mesh.devices.reshape(tuple(PARTS.values())), tuple(PARTS))
    row, col = ("yh", "yl", "xl"), ("xh", "zh", "zl")
    in_specs = (P(row, ("l",) + col), P(("l",) + row, col), P(row, col), P(row), P(col))
    return jax.shard_map(body, mesh=fine, in_specs=in_specs, out_specs=P(row, col), check_vma=False)
```
